128 devices in a mesh: db: 32 (over z, y, core), sub: 4 (over x).
Axes of the slice: x: 4, y: 4, z: 4, core: 2. Of those that a mesh axis runs over, the one named last changes fastest.
Arguments:
- codes: int32 [32768, 64], P('db', 'sub'), may hold values from 0 to 255
- tables: bfloat16 [2048, 64, 256], P('db', 'sub'), may hold values from 0.125 to 128, as said below
- limits: int32 [2048], replicated, may hold values from 3008 to 3263
Outputs:
- hit_ids: int32 [2048, 128], P(('db', 'sub'))
- hit_count: int32 [2048], P(('db', 'sub'))
The draws below stay inside these ranges and needn't reach their ends.
Inputs may be any that keep to these rules, and one draw needn't show every extreme that they name: `tables`: each value is a bfloat16 number of at least 1/8 and at most 128.
All inputs are finite; a program needn't handle non-finite values.
Results may differ from the reference program's by a relative error of at most 0.000001.
Values may be sent and summed in bfloat16 or wider, within the bound.
No kernel may reach another device: no remote copies, remote signals or barrier semaphores. Data moves between devices by JAX's collectives and lax.ppermute only.
A program may use at most 128 MiB of HBM per device.

```python
import jax
import jax.numpy as jnp
from jax import lax

M = 64
K = 256
SLOTS = 128
ROWS = 1024
Q = 2048
DB_ROWS = 32768


def nearest_centroids(key):
    return jax.random.randint(jax.random.fold_in(key, 7101), (Q, M), 0, K, dtype=jnp.int32)


def draw_tables(key, part):
    nearest = nearest_centroids(key)
    drawn = jax.random.uniform(jax.random.fold_in(key, 7201), (Q, M, K), jnp.float32, 0.125, 128.0)
    lowered = jax.random.uniform(jax.random.fold_in(key, 7204), (Q, M, K), jnp.float32, 0.125, 80.0)
    heavy = jax.random.randint(jax.random.fold_in(key, 7203), (Q,), 0, 8, dtype=jnp.int32) == 0
    values = jnp.where(heavy[:, None, None], lowered, drawn)
    lowest = jax.random.uniform(jax.random.fold_in(key, 7202), (Q, M), jnp.float32, 0.125, 16.0)
    centroid = lax.iota(jnp.int32, K)
    chosen = centroid[None, None, :] == nearest[:, :, None]
    return jnp.where(chosen, lowest[:, :, None], values).astype(jnp.bfloat16)


def draw_codes(key, part):
    nearest = nearest_centroids(key)
    ranges = DB_ROWS // ROWS
    planted_count = SLOTS + SLOTS // 2
    base = jax.random.randint(jax.random.fold_in(key, 7301), (DB_ROWS, M), 0, K, dtype=jnp.int32)
    target = jax.random.randint(jax.random.fold_in(key, 7302), (ranges,), 0, Q, dtype=jnp.int32)
    range_keys = jax.random.split(jax.random.fold_in(key, 7303), ranges)
    ranks = jax.vmap(lambda one_key: jax.random.permutation(one_key, ROWS))(range_keys)
    planted = (ranks < planted_count).reshape(DB_ROWS)
    offset = jax.random.randint(jax.random.fold_in(key, 7304), (DB_ROWS,), 0, 4, dtype=jnp.int32)
    subspace = lax.iota(jnp.int32, M)
    copied = planted[:, None] & ((subspace[None, :] + offset[:, None]) % 4 != 0)
    near_rows = jnp.repeat(nearest[target], ROWS, axis=0)
    return jnp.where(copied, near_rows, base).astype(jnp.int32)


def plant(values, own_key, smallest, top_value):
    extent = values.shape
    spot = [jax.random.randint(jax.random.fold_in(own_key, axis), (), 0, extent[axis]) for axis in range(len(extent))]
    values = values.at[tuple(spot)].set(smallest)
    longest = extent.index(max(extent))
    spot[longest] = (spot[longest] + 1) % extent[longest]
    return values.at[tuple(spot)].set(top_value)


def setup_inputs(seed: int = 0) -> dict:
    splits = jax.random.split(jax.random.key(seed), 4)
    codes = draw_codes(jax.random.fold_in(splits[3], 71), 0)
    tables = draw_tables(jax.random.fold_in(splits[3], 71), 0)
    limits = plant(jax.random.randint(splits[2], (Q,), M * 47, M * 51), jax.random.fold_in(splits[2], 1), M * 47, (M * 51) - 1).astype(jnp.int32)
    return dict(codes=codes, tables=tables, limits=limits)


def reference(codes, tables, limits):
    def add_one(index, total):
        column = lax.dynamic_index_in_dim(codes, index, 1, keepdims=False)
        table = lax.dynamic_index_in_dim(tables, index, 1, keepdims=False).astype(jnp.float32)
        return total + jnp.take(table, column, axis=1)

    distance = lax.fori_loop(0, M, add_one, jnp.zeros((Q, DB_ROWS), jnp.float32))
    matched = (distance <= limits[:, None].astype(jnp.float32)).astype(jnp.int32)
    hit_count = jnp.sum(matched, axis=1).astype(jnp.int32)
    running = jnp.cumsum(matched, axis=1).astype(jnp.int32)
    slot_index = jnp.arange(SLOTS, dtype=jnp.int32)

    def locate(row):
        return jnp.searchsorted(row, slot_index, side="right").astype(jnp.int32)

    found = jax.vmap(locate)(running)
    hit_ids = jnp.where(slot_index[None, :] < hit_count[:, None], found, -1).astype(jnp.int32)
    return hit_ids, hit_count
```

```python
import functools

import jax
import jax.numpy as jnp
from jax import lax
from jax.experimental import pallas as pl
from jax.experimental.pallas import tpu as pltpu
from jax.sharding import PartitionSpec as P

F8 = jnp.float8_e4m3fn
RANGES = 32
PARTS = 4
ROWS = 1024
QN = 64
QB = 16
K = 256
SLICE = ROWS // PARTS
CHUNK = 1024
GROUP = 8
LANES = 128
LOW_HALVES = {16: 0x0000FFFF, 8: 0x00FF00FF, 4: 0x0F0F0F0F, 2: 0x33333333, 1: 0x55555555}


def srl(word, by):
    return lax.shift_right_logical(word, jnp.full_like(word, by))


def popcount(word):
    word = word - (srl(word, 1) & 0x55555555)
    word = (word & 0x33333333) + (srl(word, 2) & 0x33333333)
    word = (word + srl(word, 4)) & 0x0F0F0F0F
    word = word + srl(word, 8)
    word = word + srl(word, 16)
    return word & 63


def lane_iota(rows):
    return lax.broadcasted_iota(jnp.int32, (rows, LANES), 1)


def picked(table, index):
    return jnp.take_along_axis(table, index, axis=1, mode="promise_in_bounds")


def exact_dot(a, b):
    return jnp.dot(
        a.astype(jnp.float32).astype(jnp.bfloat16),
        b.astype(jnp.float32).astype(jnp.bfloat16),
        preferred_element_type=jnp.float32,
    )


def pack_kernel(codes_ref, out_ref):
    rows = lax.broadcasted_iota(jnp.int32, (8, 16), 0)
    cols = lax.broadcasted_iota(jnp.int32, (8, 16), 1)
    first = 4 * (rows % 4) + 2 * (rows // 4)
    weights = jnp.where(cols == first, 1.0, jnp.where(cols == first + 1, 256.0, 0.0))
    pairs = lax.dot_general(
        weights.astype(jnp.bfloat16),
        codes_ref[...].astype(jnp.float32).astype(jnp.bfloat16),
        (((1,), (1,)), ((), ())),
        preferred_element_type=jnp.float32,
    ).astype(jnp.int32)
    words = pairs[:4] | (pairs[4:] << 16)
    pieces = []
    for part in range(PARTS):
        for word in range(4):
            for block in range(2):
                at = part * SLICE + block * LANES
                pieces.append(words[word : word + 1, at : at + LANES])
    packed = jnp.concatenate(pieces, axis=0)
    for copy in range(RANGES):
        out_ref[copy] = packed


def split_tables(tab_refs, wide_ref, hl_ref):
    for quarter, tab_ref in enumerate(tab_refs):
        wide = tab_ref[...].astype(jnp.float32).reshape(QN * 16, K)
        for side in range(2):
            wide_ref[side] = wide[:, side * LANES : (side + 1) * LANES]
        for m in range(16):
            for side in range(2):
                value = wide_ref[side, pl.ds(m, QN, stride=16), :]
                hi = value.astype(F8)
                lo = ((value - hi.astype(jnp.float32)) * 8.0).astype(F8)
                at = (quarter * 16 + m) * K + side * LANES
                hl_ref[0:QN, at : at + LANES] = hi
                hl_ref[QN : 2 * QN, at : at + LANES] = lo


def one_hot_group(words_ref, onehot_ref, chunk, quarter, first_word):
    centroid = lax.broadcasted_iota(jnp.int32, (K, LANES), 0).astype(jnp.int8)
    for block in range(CHUNK // LANES):
        source = (chunk * (CHUNK // SLICE) + block // 2) * PARTS + quarter
        for word in range(GROUP // 4):
            row = words_ref[source, pl.ds((first_word + word) * 2 + block % 2, 1), :]
            row = jnp.broadcast_to(row, (32, LANES))
            for byte in range(4):
                code = ((row >> (8 * byte)) & 255).astype(jnp.int8)
                code = jnp.concatenate([code] * (K // 32), axis=0)
                at = (word * 4 + byte) * K
                onehot_ref[at : at + K, block * LANES : (block + 1) * LANES] = jnp.where(
                    code == centroid, F8(1), F8(0)
                )


def list_hits(bits_ref, position, out_ref):
    lane = lane_iota(QN)
    halves = []
    for half in range(2):
        word = bits_ref[half]
        for step, low in LOW_HALVES.items():
            high = low << step
            high = high - (1 << 32) if high >= (1 << 31) else high
            after = pltpu.roll(word, LANES - step, 1)
            before = pltpu.roll(word, step, 1)
            word = jnp.where(
                (lane & step) == 0,
                (word & low) | ((after & low) << step),
                (word & high) | srl(before & high, step),
            )
        halves.append(word)
    counts = [popcount(word) for word in halves]
    source = lax.broadcasted_iota(jnp.int32, (LANES, LANES), 0)
    target = lax.broadcasted_iota(jnp.int32, (LANES, LANES), 1)
    order = 4 * (source % 32) + source // 32
    upto = (order <= target).astype(jnp.float32)
    sums = [exact_dot(count, upto).astype(jnp.int32) for count in counts]
    per_range = sum(
        exact_dot(counts[half], (half * 16 + order // 8 == target).astype(jnp.float32))
        for half in range(2)
    )
    first_total = jnp.broadcast_to(sums[0][:, LANES - 1 :], (QN, LANES))
    second = lane >= first_total
    base = jnp.where(second, first_total, 0)
    wanted = lane - base
    found = jnp.zeros((QN, LANES), jnp.int32)
    base = jnp.zeros((QN, LANES), jnp.int32)
    for step in (64, 32, 16, 8, 4, 2, 1):
        index = found + (step - 1)
        count = jnp.where(second, picked(sums[1], index), picked(sums[0], index))
        passed = count <= wanted
        found = jnp.where(passed, found + step, found)
        base = jnp.where(passed, count, base)
    at = 32 * (found & 3) + (found >> 2)
    word = jnp.where(second, picked(halves[1], at), picked(halves[0], at))
    rank = wanted - base
    bit = jnp.zeros((QN, LANES), jnp.int32)
    for step in (16, 8, 4, 2, 1):
        count = popcount(word & ((1 << step) - 1))
        passed = count <= rank
        rank = jnp.where(passed, rank - count, rank)
        word = jnp.where(passed, srl(word, step), word)
        bit = jnp.where(passed, bit + step, bit)
    local = jnp.where(second, 4096, 0) + 32 * found + bit
    ids = (local >> 8) * ROWS + position * SLICE + (local & (SLICE - 1))
    out_ref[:, :LANES] = ids
    out_ref[:, LANES:] = per_range.astype(jnp.int32)


def score_kernel(
    where_ref, limits_ref, words_ref, t0, t1, t2, t3, out_ref, wide_ref, hl_ref, onehot_ref, bits_ref
):
    db, sub = where_ref[0], where_ref[1]
    split_tables((t0, t1, t2, t3), wide_ref, hl_ref)
    lane = lane_iota(QN)
    mine = 64 * (db % 2) + lax.broadcasted_iota(jnp.int32, (QN, LANES), 0)
    row = jnp.broadcast_to(limits_ref[pl.ds(db // 2, 1), :], (QN, LANES)).astype(jnp.float32)
    limit = jnp.sum(jnp.where(lane == mine, row, 0.0), axis=1, keepdims=True)
    limit = jnp.broadcast_to(limit, (QN, LANES))
    bits_ref[...] = jnp.zeros_like(bits_ref)

    def score(chunk, carry):
        total = jnp.zeros((2 * QN, CHUNK), jnp.float32)
        for group in range(64 // GROUP):
            quarter = (sub + PARTS - group // 2) % PARTS
            one_hot_group(words_ref, onehot_ref, chunk, quarter, (group % 2) * (GROUP // 4))
            at = group * GROUP * K
            total = total + jnp.dot(
                hl_ref[:, at : at + GROUP * K],
                onehot_ref[...],
                preferred_element_type=jnp.float32,
            )
        distance = total[:QN] + total[QN:] * 0.125
        bits = jnp.zeros((QN, LANES), jnp.int32)
        for block in range(CHUNK // LANES):
            matched = distance[:, block * LANES : (block + 1) * LANES] <= limit
            bits = bits | jnp.where(matched, 1 << block, 0)
        half = chunk // 4
        bits_ref[half] = bits_ref[half] | (bits << (8 * (chunk % 4)))
        return carry

    lax.fori_loop(0, RANGES * SLICE // CHUNK, score, 0)
    list_hits(bits_ref, sub, out_ref)


def merge_kernel(lists_ref, ids_ref, count_ref):
    lane = lane_iota(QB)
    source = lax.broadcasted_iota(jnp.int32, (LANES, LANES), 0)
    segment = lax.broadcasted_iota(jnp.int32, (LANES, LANES), 1)
    lists = [lists_ref[pl.ds(x * QB, QB), :LANES] for x in range(PARTS)]
    counts = [lists_ref[pl.ds(x * QB, QB), LANES:] for x in range(PARTS)]
    ends = jnp.zeros((QB, LANES), jnp.float32)
    skipped = jnp.zeros((QB, LANES), jnp.float32)
    totals = jnp.zeros((8, QB), jnp.float32)
    for x in range(PARTS):
        upto = (4 * source + x <= segment).astype(jnp.float32)
        ends = ends + exact_dot(counts[x], upto)
        ahead = ((segment % 4 == x) & (source < segment // 4)).astype(jnp.float32)
        skipped = skipped + exact_dot(counts[x], ahead)
        totals = totals + lax.dot_general(
            jnp.ones((8, LANES), jnp.bfloat16),
            counts[x].astype(jnp.float32).astype(jnp.bfloat16),
            (((1,), (1,)), ((), ())),
            preferred_element_type=jnp.float32,
        )
    ends = ends.astype(jnp.int32)
    skipped = skipped.astype(jnp.int32)
    found = jnp.zeros((QB, LANES), jnp.int32)
    base = jnp.zeros((QB, LANES), jnp.int32)
    for step in (64, 32, 16, 8, 4, 2, 1):
        count = picked(ends, found + (step - 1))
        passed = count <= lane
        found = jnp.where(passed, found + step, found)
        base = jnp.where(passed, count, base)
    valid = lane < jnp.broadcast_to(ends[:, LANES - 1 :], (QB, LANES))
    index = lane - base + picked(skipped, found)
    index = jnp.where(valid, index, 0)
    value = jnp.zeros((QB, LANES), jnp.int32)
    for x in range(PARTS):
        value = jnp.where(found % 4 == x, picked(lists[x], index), value)
    ids_ref[...] = jnp.where(valid, value, -1)
    count_ref[...] = totals[:1].astype(jnp.int32)


VMEM = pl.BlockSpec(memory_space=pltpu.VMEM)
SMEM = pl.BlockSpec(memory_space=pltpu.SMEM)
PARAMS = pltpu.CompilerParams(vmem_limit_bytes=48 * 2**20)


def pack(codes):
    return pl.pallas_call(
        pack_kernel,
        out_shape=jax.ShapeDtypeStruct((RANGES, PARTS * 8, LANES), jnp.int32),
        in_specs=[VMEM],
        out_specs=VMEM,
        compiler_params=PARAMS,
        name="pack",
    )(codes)


def score(where, limits, words, tabs):
    return pl.pallas_call(
        score_kernel,
        out_shape=jax.ShapeDtypeStruct((QN, 2 * LANES), jnp.int32),
        in_specs=[SMEM] + [VMEM] * 6,
        out_specs=VMEM,
        scratch_shapes=[
            pltpu.VMEM((2, QN * 16, LANES), jnp.float32),
            pltpu.VMEM((2 * QN, 64 * K), F8),
            pltpu.VMEM((GROUP * K, CHUNK), F8),
            pltpu.VMEM((2, QN, LANES), jnp.int32),
        ],
        compiler_params=PARAMS,
        name="score",
    )(where, limits, words, *tabs)


def merge(lists):
    return pl.pallas_call(
        merge_kernel,
        out_shape=(
            jax.ShapeDtypeStruct((QB, LANES), jnp.int32),
            jax.ShapeDtypeStruct((1, QB), jnp.int32),
        ),
        in_specs=[VMEM],
        out_specs=(VMEM, VMEM),
        compiler_params=PARAMS,
        name="merge",
    )(lists)


def per_device(codes, tables, limits):
    where = jnp.stack([lax.axis_index("db"), lax.axis_index("sub")]).astype(jnp.int32)
    shifted = [
        lax.ppermute(tables, "sub", [(x, (x + k) % PARTS) for x in range(PARTS)])
        for k in range(1, PARTS)
    ]
    sent = pack(codes).reshape(RANGES * PARTS, 8, LANES)
    words = lax.all_to_all(sent, ("db", "sub"), split_axis=0, concat_axis=0, tiled=True)
    lists = score(where, limits.reshape(16, LANES), words, [tables] + shifted)
    received = lax.all_to_all(lists, "sub", split_axis=0, concat_axis=0, tiled=True)
    ids, count = merge(received)
    return ids, count.reshape(QB)


def solution(mesh):
    placed = (P("db", "sub"), P("db", "sub", None), P())
    return jax.shard_map(
        per_device,
        mesh=mesh,
        in_specs=placed,
        out_specs=(P(("db", "sub"), None), P(("db", "sub"))),
        check_vma=False,
    )
```

```python
import functools

import jax
import jax.numpy as jnp
from jax import lax
from jax.experimental import pallas as pl
from jax.experimental.pallas import tpu as pltpu
from jax.sharding import PartitionSpec as P

F8 = jnp.float8_e4m3fn
RANGES = 32
PARTS = 4
ROWS = 1024
QN = 64
QB = 16
K = 256
SLICE = ROWS // PARTS
CHUNK = 1024
GROUP = 8
LANES = 128
LOW_HALVES = {16: 0x0000FFFF, 8: 0x00FF00FF, 4: 0x0F0F0F0F, 2: 0x33333333, 1: 0x55555555}


def srl(word, by):
    return lax.shift_right_logical(word, jnp.full_like(word, by))


def popcount(word):
    word = word - (srl(word, 1) & 0x55555555)
    word = (word & 0x33333333) + (srl(word, 2) & 0x33333333)
    word = (word + srl(word, 4)) & 0x0F0F0F0F
    word = word + srl(word, 8)
    word = word + srl(word, 16)
    return word & 63


def lane_iota(rows):
    return lax.broadcasted_iota(jnp.int32, (rows, LANES), 1)


def picked(table, index):
    return jnp.take_along_axis(table, index, axis=1, mode="promise_in_bounds")


def exact_dot(a, b):
    return jnp.dot(
        a.astype(jnp.float32).astype(jnp.bfloat16),
        b.astype(jnp.float32).astype(jnp.bfloat16),
        preferred_element_type=jnp.float32,
    )


def pack_kernel(codes_ref, out_ref):
    rows = lax.broadcasted_iota(jnp.int32, (8, 16), 0)
    cols = lax.broadcasted_iota(jnp.int32, (8, 16), 1)
    first = 4 * (rows % 4) + 2 * (rows // 4)
    weights = jnp.where(cols == first, 1.0, jnp.where(cols == first + 1, 256.0, 0.0))
    pairs = lax.dot_general(
        weights.astype(jnp.bfloat16),
        codes_ref[...].astype(jnp.float32).astype(jnp.bfloat16),
        (((1,), (1,)), ((), ())),
        preferred_element_type=jnp.float32,
    ).astype(jnp.int32)
    words = pairs[:4] | (pairs[4:] << 16)
    pieces = []
    for part in range(PARTS):
        for word in range(4):
            for block in range(2):
                at = part * SLICE + block * LANES
                pieces.append(words[word : word + 1, at : at + LANES])
    packed = jnp.concatenate(pieces, axis=0)
    for copy in range(RANGES):
        out_ref[copy] = packed


def split_tables(tab_refs, wide_ref, hl_ref):
    own, before, after, far_low, far_high = tab_refs
    for quarter, halves in enumerate(((own,), (before,), (far_low, far_high), (after,))):
        wide = jnp.concatenate(
            [ref[...].astype(jnp.float32).reshape(-1, K) for ref in halves], axis=0
        )
        for side in range(2):
            wide_ref[side] = wide[:, side * LANES : (side + 1) * LANES]
        for m in range(16):
            for side in range(2):
                value = wide_ref[side, pl.ds(m, QN, stride=16), :]
                hi = value.astype(F8)
                lo = ((value - hi.astype(jnp.float32)) * 8.0).astype(F8)
                at = (quarter * 16 + m) * K + side * LANES
                hl_ref[0:QN, at : at + LANES] = hi
                hl_ref[QN : 2 * QN, at : at + LANES] = lo


def one_hot_group(words_ref, onehot_ref, chunk, quarter, first_word):
    centroid = lax.broadcasted_iota(jnp.int32, (K, LANES), 0).astype(jnp.int8)
    for block in range(CHUNK // LANES):
        source = (chunk * (CHUNK // SLICE) + block // 2) * PARTS + quarter
        for word in range(GROUP // 4):
            row = words_ref[source, pl.ds((first_word + word) * 2 + block % 2, 1), :]
            row = jnp.broadcast_to(row, (32, LANES))
            for byte in range(4):
                code = ((row >> (8 * byte)) & 255).astype(jnp.int8)
                code = jnp.concatenate([code] * (K // 32), axis=0)
                at = (word * 4 + byte) * K
                onehot_ref[at : at + K, block * LANES : (block + 1) * LANES] = jnp.where(
                    code == centroid, F8(1), F8(0)
                )


def list_hits(bits_ref, position, out_ref):
    lane = lane_iota(QN)
    halves = []
    for half in range(2):
        word = bits_ref[half]
        for step, low in LOW_HALVES.items():
            high = low << step
            high = high - (1 << 32) if high >= (1 << 31) else high
            after = pltpu.roll(word, LANES - step, 1)
            before = pltpu.roll(word, step, 1)
            word = jnp.where(
                (lane & step) == 0,
                (word & low) | ((after & low) << step),
                (word & high) | srl(before & high, step),
            )
        halves.append(word)
    counts = [popcount(word) for word in halves]
    source = lax.broadcasted_iota(jnp.int32, (LANES, LANES), 0)
    target = lax.broadcasted_iota(jnp.int32, (LANES, LANES), 1)
    order = 4 * (source % 32) + source // 32
    upto = (order <= target).astype(jnp.float32)
    sums = [exact_dot(count, upto).astype(jnp.int32) for count in counts]
    per_range = sum(
        exact_dot(counts[half], (half * 16 + order // 8 == target).astype(jnp.float32))
        for half in range(2)
    )
    first_total = jnp.broadcast_to(sums[0][:, LANES - 1 :], (QN, LANES))
    second = lane >= first_total
    base = jnp.where(second, first_total, 0)
    wanted = lane - base
    found = jnp.zeros((QN, LANES), jnp.int32)
    base = jnp.zeros((QN, LANES), jnp.int32)
    for step in (64, 32, 16, 8, 4, 2, 1):
        index = found + (step - 1)
        count = jnp.where(second, picked(sums[1], index), picked(sums[0], index))
        passed = count <= wanted
        found = jnp.where(passed, found + step, found)
        base = jnp.where(passed, count, base)
    at = 32 * (found & 3) + (found >> 2)
    word = jnp.where(second, picked(halves[1], at), picked(halves[0], at))
    rank = wanted - base
    bit = jnp.zeros((QN, LANES), jnp.int32)
    for step in (16, 8, 4, 2, 1):
        count = popcount(word & ((1 << step) - 1))
        passed = count <= rank
        rank = jnp.where(passed, rank - count, rank)
        word = jnp.where(passed, srl(word, step), word)
        bit = jnp.where(passed, bit + step, bit)
    local = jnp.where(second, 4096, 0) + 32 * found + bit
    ids = (local >> 8) * ROWS + position * SLICE + (local & (SLICE - 1))
    out_ref[:, :LANES] = ids
    out_ref[:, LANES:] = per_range.astype(jnp.int32)


def score_kernel(
    where_ref, limits_ref, words_ref, t0, t1, t2, t3, t4, out_ref, wide_ref, hl_ref, onehot_ref, bits_ref
):
    db, sub = where_ref[0], where_ref[1]
    split_tables((t0, t1, t2, t3, t4), wide_ref, hl_ref)
    lane = lane_iota(QN)
    mine = 64 * (db % 2) + lax.broadcasted_iota(jnp.int32, (QN, LANES), 0)
    row = jnp.broadcast_to(limits_ref[pl.ds(db // 2, 1), :], (QN, LANES)).astype(jnp.float32)
    limit = jnp.sum(jnp.where(lane == mine, row, 0.0), axis=1, keepdims=True)
    limit = jnp.broadcast_to(limit, (QN, LANES))
    bits_ref[...] = jnp.zeros_like(bits_ref)

    def score(chunk, carry):
        total = jnp.zeros((2 * QN, CHUNK), jnp.float32)
        for group in range(64 // GROUP):
            quarter = (sub + PARTS - group // 2) % PARTS
            one_hot_group(words_ref, onehot_ref, chunk, quarter, (group % 2) * (GROUP // 4))
            at = group * GROUP * K
            total = total + jnp.dot(
                hl_ref[:, at : at + GROUP * K],
                onehot_ref[...],
                preferred_element_type=jnp.float32,
            )
        distance = total[:QN] + total[QN:] * 0.125
        bits = jnp.zeros((QN, LANES), jnp.int32)
        for block in range(CHUNK // LANES):
            matched = distance[:, block * LANES : (block + 1) * LANES] <= limit
            bits = bits | jnp.where(matched, 1 << block, 0)
        half = chunk // 4
        bits_ref[half] = bits_ref[half] | (bits << (8 * (chunk % 4)))
        return carry

    lax.fori_loop(0, RANGES * SLICE // CHUNK, score, 0)
    list_hits(bits_ref, sub, out_ref)


def merge_kernel(lists_ref, ids_ref, count_ref):
    lane = lane_iota(QB)
    source = lax.broadcasted_iota(jnp.int32, (LANES, LANES), 0)
    segment = lax.broadcasted_iota(jnp.int32, (LANES, LANES), 1)
    lists = [lists_ref[pl.ds(x * QB, QB), :LANES] for x in range(PARTS)]
    counts = [lists_ref[pl.ds(x * QB, QB), LANES:] for x in range(PARTS)]
    ends = jnp.zeros((QB, LANES), jnp.float32)
    skipped = jnp.zeros((QB, LANES), jnp.float32)
    totals = jnp.zeros((8, QB), jnp.float32)
    for x in range(PARTS):
        upto = (4 * source + x <= segment).astype(jnp.float32)
        ends = ends + exact_dot(counts[x], upto)
        ahead = ((segment % 4 == x) & (source < segment // 4)).astype(jnp.float32)
        skipped = skipped + exact_dot(counts[x], ahead)
        totals = totals + lax.dot_general(
            jnp.ones((8, LANES), jnp.bfloat16),
            counts[x].astype(jnp.float32).astype(jnp.bfloat16),
            (((1,), (1,)), ((), ())),
            preferred_element_type=jnp.float32,
        )
    ends = ends.astype(jnp.int32)
    skipped = skipped.astype(jnp.int32)
    found = jnp.zeros((QB, LANES), jnp.int32)
    base = jnp.zeros((QB, LANES), jnp.int32)
    for step in (64, 32, 16, 8, 4, 2, 1):
        count = picked(ends, found + (step - 1))
        passed = count <= lane
        found = jnp.where(passed, found + step, found)
        base = jnp.where(passed, count, base)
    valid = lane < jnp.broadcast_to(ends[:, LANES - 1 :], (QB, LANES))
    index = lane - base + picked(skipped, found)
    index = jnp.where(valid, index, 0)
    value = jnp.zeros((QB, LANES), jnp.int32)
    for x in range(PARTS):
        value = jnp.where(found % 4 == x, picked(lists[x], index), value)
    ids_ref[...] = jnp.where(valid, value, -1)
    count_ref[...] = totals[:1].astype(jnp.int32)


VMEM = pl.BlockSpec(memory_space=pltpu.VMEM)
SMEM = pl.BlockSpec(memory_space=pltpu.SMEM)
PARAMS = pltpu.CompilerParams(vmem_limit_bytes=48 * 2**20)


def pack(codes):
    return pl.pallas_call(
        pack_kernel,
        out_shape=jax.ShapeDtypeStruct((RANGES, PARTS * 8, LANES), jnp.int32),
        in_specs=[VMEM],
        out_specs=VMEM,
        compiler_params=PARAMS,
        name="pack",
    )(codes)


def score(where, limits, words, tabs):
    return pl.pallas_call(
        score_kernel,
        out_shape=jax.ShapeDtypeStruct((QN, 2 * LANES), jnp.int32),
        in_specs=[SMEM] + [VMEM] * 7,
        out_specs=VMEM,
        scratch_shapes=[
            pltpu.VMEM((2, QN * 16, LANES), jnp.float32),
            pltpu.VMEM((2 * QN, 64 * K), F8),
            pltpu.VMEM((GROUP * K, CHUNK), F8),
            pltpu.VMEM((2, QN, LANES), jnp.int32),
        ],
        compiler_params=PARAMS,
        name="score",
    )(where, limits, words, *tabs)


def merge(lists):
    return pl.pallas_call(
        merge_kernel,
        out_shape=(
            jax.ShapeDtypeStruct((QB, LANES), jnp.int32),
            jax.ShapeDtypeStruct((1, QB), jnp.int32),
        ),
        in_specs=[VMEM],
        out_specs=(VMEM, VMEM),
        compiler_params=PARAMS,
        name="merge",
    )(lists)


def shifted(array, by):
    return lax.ppermute(array, "sub", [(x, (x + by) % PARTS) for x in range(PARTS)])


def per_device(codes, tables, limits):
    where = jnp.stack([lax.axis_index("db"), lax.axis_index("sub")]).astype(jnp.int32)
    before, after = shifted(tables, 1), shifted(tables, -1)
    far_low = shifted(before[: QN // 2], 1)
    far_high = shifted(after[QN // 2 :], -1)
    sent = pack(codes).reshape(RANGES * PARTS, 8, LANES)
    words = lax.all_to_all(sent, ("db", "sub"), split_axis=0, concat_axis=0, tiled=True)
    lists = score(where, limits.reshape(16, LANES), words, (tables, before, after, far_low, far_high))
    received = lax.all_to_all(lists, "sub", split_axis=0, concat_axis=0, tiled=True)
    ids, count = merge(received)
    return ids, count.reshape(QB)


def solution(mesh):
    placed = (P("db", "sub"), P("db", "sub", None), P())
    return jax.shard_map(
        per_device,
        mesh=mesh,
        in_specs=placed,
        out_specs=(P(("db", "sub"), None), P(("db", "sub"))),
        check_vma=False,
    )
```

```python
import functools

import jax
import jax.numpy as jnp
from jax import lax
from jax.experimental import pallas as pl
from jax.experimental.pallas import tpu as pltpu
from jax.sharding import PartitionSpec as P

F8 = jnp.float8_e4m3fn
RANGES = 32
PARTS = 4
ROWS = 1024
QN = 64
QB = 16
K = 256
SLICE = ROWS // PARTS
CHUNK = 2048
GROUP = 4
LANES = 128
LOW_HALVES = {16: 0x0000FFFF, 8: 0x00FF00FF, 4: 0x0F0F0F0F, 2: 0x33333333, 1: 0x55555555}


def srl(word, by):
    return lax.shift_right_logical(word, jnp.full_like(word, by))


def popcount(word):
    word = word - (srl(word, 1) & 0x55555555)
    word = (word & 0x33333333) + (srl(word, 2) & 0x33333333)
    word = (word + srl(word, 4)) & 0x0F0F0F0F
    word = word + srl(word, 8)
    word = word + srl(word, 16)
    return word & 63


def lane_iota(rows):
    return lax.broadcasted_iota(jnp.int32, (rows, LANES), 1)


def picked(table, index):
    return jnp.take_along_axis(table, index, axis=1, mode="promise_in_bounds")


def exact_dot(a, b):
    return jnp.dot(
        a.astype(jnp.float32).astype(jnp.bfloat16),
        b.astype(jnp.float32).astype(jnp.bfloat16),
        preferred_element_type=jnp.float32,
    )


def pack_kernel(codes_ref, out_ref):
    codes = codes_ref[...]
    words = [
        codes[4 * word : 4 * word + 1]
        | (codes[4 * word + 1 : 4 * word + 2] << 8)
        | (codes[4 * word + 2 : 4 * word + 3] << 16)
        | (codes[4 * word + 3 : 4 * word + 4] << 24)
        for word in range(4)
    ]
    pieces = []
    for part in range(PARTS):
        for word in range(4):
            for side in range(2):
                at = part * SLICE + side * LANES
                pieces.append(words[word][:, at : at + LANES])
    packed = jnp.concatenate(pieces, axis=0)
    for copy in range(RANGES):
        out_ref[copy] = packed


def split_tables(tab_refs, wide_ref, hl_ref):
    wide = jnp.concatenate([ref[...].astype(jnp.float32).reshape(-1, K) for ref in tab_refs], axis=0)
    for side in range(2):
        wide_ref[side] = wide[:, side * LANES : (side + 1) * LANES]
    for m in range(16):
        for side in range(2):
            value = wide_ref[side, pl.ds(m, QN, stride=16), :]
            hi = value.astype(F8)
            lo = ((value - hi.astype(jnp.float32)) * 8.0).astype(F8)
            at = m * K + side * LANES
            hl_ref[0:QN, at : at + LANES] = hi
            hl_ref[QN : 2 * QN, at : at + LANES] = lo


def split_kernel(own_ref, before_ref, after_ref, hl0, hl1, hl3, wide_ref):
    split_tables((own_ref,), wide_ref, hl0)
    split_tables((before_ref,), wide_ref, hl1)
    split_tables((after_ref,), wide_ref, hl3)


def one_hot_group(words_ref, onehot_ref, chunk, quarter, first_word):
    centroid = lax.broadcasted_iota(jnp.int32, (K, LANES), 0).astype(jnp.int8)
    for block in range(CHUNK // LANES):
        source = (chunk * (CHUNK // SLICE) + block // 2) * PARTS + quarter
        for word in range(GROUP // 4):
            row = words_ref[source, pl.ds((first_word + word) * 2 + block % 2, 1), :]
            row = jnp.broadcast_to(row, (32, LANES))
            for byte in range(4):
                code = ((row >> (8 * byte)) & 255).astype(jnp.int8)
                code = jnp.concatenate([code] * (K // 32), axis=0)
                at = (word * 4 + byte) * K
                onehot_ref[at : at + K, block * LANES : (block + 1) * LANES] = jnp.where(
                    code == centroid, F8(1), F8(0)
                )


def hit_words(word, half):
    lane = lane_iota(QN)
    for step, low in LOW_HALVES.items():
        high = low << step
        high = high - (1 << 32) if high >= (1 << 31) else high
        after = pltpu.roll(word, LANES - step, 1)
        before = pltpu.roll(word, step, 1)
        word = jnp.where(
            (lane & step) == 0,
            (word & low) | ((after & low) << step),
            (word & high) | srl(before & high, step),
        )
    count = popcount(word)
    source = lax.broadcasted_iota(jnp.int32, (LANES, LANES), 0)
    target = lax.broadcasted_iota(jnp.int32, (LANES, LANES), 1)
    order = 4 * (source % 32) + source // 32
    ends = exact_dot(count, (order <= target).astype(jnp.float32)).astype(jnp.int32)
    in_range = half * 16 + order // 8 == target % RANGES
    return word, ends, exact_dot(count, in_range.astype(jnp.float32))


def list_hits(halves, position):
    lane = lane_iota(QN)
    (first_word, first_ends, first_hits), (last_word, last_ends, last_hits) = halves
    first_total = jnp.broadcast_to(first_ends[:, LANES - 1 :], (QN, LANES))
    second = lane >= first_total
    wanted = jnp.where(second, lane - first_total, lane)
    found = jnp.zeros((QN, LANES), jnp.int32)
    base = jnp.zeros((QN, LANES), jnp.int32)
    for step in (64, 32, 16, 8, 4, 2, 1):
        index = found + (step - 1)
        count = jnp.where(second, picked(last_ends, index), picked(first_ends, index))
        passed = count <= wanted
        found = jnp.where(passed, found + step, found)
        base = jnp.where(passed, count, base)
    at = 32 * (found & 3) + (found >> 2)
    word = jnp.where(second, picked(last_word, at), picked(first_word, at))
    rank = wanted - base
    bit = jnp.zeros((QN, LANES), jnp.int32)
    for step in (16, 8, 4, 2, 1):
        count = popcount(word & ((1 << step) - 1))
        passed = count <= rank
        rank = jnp.where(passed, rank - count, rank)
        word = jnp.where(passed, srl(word, step), word)
        bit = jnp.where(passed, bit + step, bit)
    local = jnp.where(second, 4096, 0) + 32 * found + bit
    ids = (local >> 8) * ROWS + position * SLICE + (local & (SLICE - 1))
    return ids, (first_hits + last_hits).astype(jnp.int32)


def score_kernel(
    limits_ref,
    words_ref,
    hl0,
    hl1_hbm,
    hl3_hbm,
    far_low_hbm,
    far_high_hbm,
    out0,
    out1,
    out2,
    out3,
    far_low,
    far_high,
    wide_ref,
    hl1,
    hl3,
    hl2,
    onehot_ref,
    lists_ref,
    copied,
):
    moves = ((hl1_hbm, hl1), (hl3_hbm, hl3), (far_low_hbm, far_low), (far_high_hbm, far_high))
    copies = [
        pltpu.make_async_copy(source, target, copied.at[at])
        for at, (source, target) in enumerate(moves)
    ]
    for copy in copies:
        copy.start()
    db, sub = lax.axis_index("db"), lax.axis_index("sub")
    lane = lane_iota(QN)
    mine = 64 * (db % 2) + lax.broadcasted_iota(jnp.int32, (QN, LANES), 0)
    row = jnp.broadcast_to(limits_ref[pl.ds(db // 2, 1), :], (QN, LANES)).astype(jnp.float32)
    limit = jnp.sum(jnp.where(lane == mine, row, 0.0), axis=1, keepdims=True)
    limit = jnp.broadcast_to(limit, (QN, LANES))

    halves = []
    bits = jnp.zeros((QN, LANES), jnp.int32)
    for chunk in range(RANGES * SLICE // CHUNK):
        total = jnp.zeros((2 * QN, CHUNK), jnp.float32)
        for group in range(64 // GROUP):
            shift = (0, 1, 3, 2)[group // 4]
            hl_ref = (hl0, hl1, hl2, hl3)[shift]
            if chunk == 0 and group in (4, 8):
                copies[group // 4 - 1].wait()
            if chunk == 0 and group == 12:
                copies[2].wait()
                copies[3].wait()
                split_tables((far_low, far_high), wide_ref, hl2)
            quarter = (sub + PARTS - shift) % PARTS
            one_hot_group(words_ref, onehot_ref, chunk, quarter, (group % 4) * (GROUP // 4))
            at = (group % 4) * GROUP * K
            total = total + jnp.dot(
                hl_ref[:, at : at + GROUP * K],
                onehot_ref[...],
                preferred_element_type=jnp.float32,
            )
        distance = total[:QN] + total[QN:] * 0.125
        for block in range(CHUNK // LANES):
            matched = distance[:, block * LANES : (block + 1) * LANES] <= limit
            at = (chunk * (CHUNK // LANES) + block) % 32
            bits = bits | jnp.where(matched, (1 << at) if at < 31 else -(1 << 31), 0)
        if (chunk + 1) * CHUNK % 4096 == 0:
            halves.append(hit_words(bits, len(halves)))
            bits = jnp.zeros((QN, LANES), jnp.int32)
    ids, hits = list_hits(halves, sub)
    lists_ref[:, :LANES] = ids
    lists_ref[:, LANES:] = hits
    for shift, out_ref in enumerate((out0, out1, out2, out3)):
        owner = (sub + shift) % PARTS
        out_ref[...] = lists_ref[pl.ds(pl.multiple_of(owner * QB, QB), QB), :]


def merge_kernel(l0, l1, l2, l3, ids_ref, count_ref):
    lane = lane_iota(QB)
    slices = [(lax.axis_index("sub") + PARTS - shift) % PARTS for shift in range(PARTS)]
    refs = (l0, l1, l2, l3)
    counts = jnp.zeros((QB, LANES), jnp.int32)
    for x, ref in zip(slices, refs):
        counts = jnp.where(lane // RANGES == x, ref[:, LANES:], counts)
    source = lax.broadcasted_iota(jnp.int32, (LANES, LANES), 0)
    segment = lax.broadcasted_iota(jnp.int32, (LANES, LANES), 1)
    order = 4 * (source % RANGES) + source // RANGES
    ends = exact_dot(counts, (order <= segment).astype(jnp.float32)).astype(jnp.int32)
    ahead = (order % 4 == segment % 4) & (order < segment)
    skipped = exact_dot(counts, ahead.astype(jnp.float32)).astype(jnp.int32)
    totals = lax.dot_general(
        jnp.ones((8, LANES), jnp.bfloat16),
        counts.astype(jnp.float32).astype(jnp.bfloat16),
        (((1,), (1,)), ((), ())),
        preferred_element_type=jnp.float32,
    )
    found = jnp.zeros((QB, LANES), jnp.int32)
    base = jnp.zeros((QB, LANES), jnp.int32)
    for step in (64, 32, 16, 8, 4, 2, 1):
        count = picked(ends, found + (step - 1))
        passed = count <= lane
        found = jnp.where(passed, found + step, found)
        base = jnp.where(passed, count, base)
    valid = lane < jnp.broadcast_to(ends[:, LANES - 1 :], (QB, LANES))
    index = jnp.where(valid, lane - base + picked(skipped, found), 0)
    value = jnp.zeros((QB, LANES), jnp.int32)
    for x, ref in zip(slices, refs):
        value = jnp.where(found % 4 == x, picked(ref[:, :LANES], index), value)
    ids_ref[...] = jnp.where(valid, value, -1)
    count_ref[...] = totals[:1].astype(jnp.int32)


VMEM = pl.BlockSpec(memory_space=pltpu.VMEM)
ANY = pl.BlockSpec(memory_space=pl.ANY)
PARAMS = pltpu.CompilerParams(vmem_limit_bytes=20 * 2**20)


def pack(codes):
    return pl.pallas_call(
        pack_kernel,
        out_shape=jax.ShapeDtypeStruct((RANGES, PARTS * 8, LANES), jnp.int32),
        in_specs=[VMEM],
        out_specs=VMEM,
        compiler_params=PARAMS,
        name="pack",
    )(codes.T)


def split(own, before, after):
    return pl.pallas_call(
        split_kernel,
        out_shape=[jax.ShapeDtypeStruct((2 * QN, 16 * K), F8)] * 3,
        in_specs=[VMEM] * 3,
        out_specs=[VMEM] * 3,
        scratch_shapes=[pltpu.VMEM((2, QN * 16, LANES), jnp.float32)],
        compiler_params=PARAMS,
        name="split",
    )(own, before, after)


def score(limits, words, tabs):
    return pl.pallas_call(
        score_kernel,
        out_shape=[jax.ShapeDtypeStruct((QB, 2 * LANES), jnp.int32)] * PARTS,
        in_specs=[VMEM] * 3 + [ANY] * 4,
        out_specs=[VMEM] * PARTS,
        scratch_shapes=[
            pltpu.VMEM((QN // 2, 16, K), jnp.bfloat16),
            pltpu.VMEM((QN // 2, 16, K), jnp.bfloat16),
            pltpu.VMEM((2, QN * 16, LANES), jnp.float32),
            pltpu.VMEM((2 * QN, 16 * K), F8),
            pltpu.VMEM((2 * QN, 16 * K), F8),
            pltpu.VMEM((2 * QN, 16 * K), F8),
            pltpu.VMEM((GROUP * K, CHUNK), F8),
            pltpu.VMEM((QN, 2 * LANES), jnp.int32),
            pltpu.SemaphoreType.DMA((4,)),
        ],
        compiler_params=PARAMS,
        name="score",
    )(limits, words, *tabs)


def merge(lists):
    return pl.pallas_call(
        merge_kernel,
        out_shape=(
            jax.ShapeDtypeStruct((QB, LANES), jnp.int32),
            jax.ShapeDtypeStruct((1, QB), jnp.int32),
        ),
        in_specs=[VMEM] * PARTS,
        out_specs=(VMEM, VMEM),
        compiler_params=PARAMS,
        name="merge",
    )(*lists)


def shifted(array, by):
    return lax.ppermute(array, "sub", [(x, (x + by) % PARTS) for x in range(PARTS)])


def per_device(codes, tables, limits):
    before, after = shifted(tables, 1), shifted(tables, -1)
    far_low = shifted(before[: QN // 2], 1)
    far_high = shifted(after[QN // 2 :], -1)
    sent = pack(codes).reshape(RANGES * PARTS, 8, LANES)
    words = lax.all_to_all(sent, ("db", "sub"), split_axis=0, concat_axis=0, tiled=True)
    lists = score(
        limits.reshape(16, LANES), words, (*split(tables, before, after), far_low, far_high)
    )
    received = [lists[0]] + [shifted(lists[k], k) for k in range(1, PARTS)]
    ids, count = merge(received)
    return ids, count.reshape(QB)


def solution(mesh):
    placed = (P("db", "sub"), P("db", "sub", None), P())
    return jax.shard_map(
        per_device,
        mesh=mesh,
        in_specs=placed,
        out_specs=(P(("db", "sub"), None), P(("db", "sub"))),
        check_vma=False,
    )
```

```python
import functools

import jax
import jax.numpy as jnp
from jax import lax
from jax.experimental import pallas as pl
from jax.experimental.pallas import tpu as pltpu
from jax.sharding import PartitionSpec as P

F8 = jnp.float8_e4m3fn
RANGES = 32
PARTS = 4
ROWS = 1024
QN = 64
QB = 16
K = 256
SLICE = ROWS // PARTS
CHUNK = 2048
GROUP = 4
LANES = 128
LOW_HALVES = {16: 0x0000FFFF, 8: 0x00FF00FF, 4: 0x0F0F0F0F, 2: 0x33333333, 1: 0x55555555}


def srl(word, by):
    return lax.shift_right_logical(word, jnp.full_like(word, by))


def popcount(word):
    word = word - (srl(word, 1) & 0x55555555)
    word = (word & 0x33333333) + (srl(word, 2) & 0x33333333)
    word = (word + srl(word, 4)) & 0x0F0F0F0F
    word = word + srl(word, 8)
    word = word + srl(word, 16)
    return word & 63


def lane_iota(rows):
    return lax.broadcasted_iota(jnp.int32, (rows, LANES), 1)


def picked(table, index):
    return jnp.take_along_axis(table, index, axis=1, mode="promise_in_bounds")


def exact_dot(a, b):
    return jnp.dot(
        a.astype(jnp.float32).astype(jnp.bfloat16),
        b.astype(jnp.float32).astype(jnp.bfloat16),
        preferred_element_type=jnp.float32,
    )


def pack_kernel(codes_ref, out_ref):
    codes = codes_ref[...]
    words = [
        codes[4 * word : 4 * word + 1]
        | (codes[4 * word + 1 : 4 * word + 2] << 8)
        | (codes[4 * word + 2 : 4 * word + 3] << 16)
        | (codes[4 * word + 3 : 4 * word + 4] << 24)
        for word in range(4)
    ]
    pieces = []
    for part in range(PARTS):
        for word in range(4):
            for side in range(2):
                at = part * SLICE + side * LANES
                pieces.append(words[word][:, at : at + LANES])
    packed = jnp.concatenate(pieces, axis=0)
    for copy in range(RANGES):
        out_ref[copy] = packed


def split_tables(tab_refs, wide_ref, hl_ref):
    wide = jnp.concatenate([ref[...].astype(jnp.float32).reshape(-1, K) for ref in tab_refs], axis=0)
    for side in range(2):
        wide_ref[side] = wide[:, side * LANES : (side + 1) * LANES]
    for m in range(16):
        for side in range(2):
            value = wide_ref[side, pl.ds(m, QN, stride=16), :]
            hi = value.astype(F8)
            lo = ((value - hi.astype(jnp.float32)) * 8.0).astype(F8)
            at = m * K + side * LANES
            hl_ref[0:QN, at : at + LANES] = hi
            hl_ref[QN : 2 * QN, at : at + LANES] = lo


def split_kernel(own_ref, before_ref, after_ref, hl0, hl1, hl3, wide_ref):
    split_tables((own_ref,), wide_ref, hl0)
    split_tables((before_ref,), wide_ref, hl1)
    split_tables((after_ref,), wide_ref, hl3)


def one_hot_group(words_ref, onehot_ref, chunk, quarter, first_word):
    centroid = lax.broadcasted_iota(jnp.int32, (K, LANES), 0).astype(jnp.int8)
    for block in range(CHUNK // LANES):
        source = (chunk * (CHUNK // SLICE) + block // 2) * PARTS + quarter
        for word in range(GROUP // 4):
            row = words_ref[source, pl.ds((first_word + word) * 2 + block % 2, 1), :]
            row = jnp.broadcast_to(row, (32, LANES))
            for byte in range(4):
                code = ((row >> (8 * byte)) & 255).astype(jnp.int8)
                code = jnp.concatenate([code] * (K // 32), axis=0)
                at = (word * 4 + byte) * K
                onehot_ref[at : at + K, block * LANES : (block + 1) * LANES] = jnp.where(
                    code == centroid, F8(1), F8(0)
                )


def hit_words(word, half):
    lane = lane_iota(QN)
    for step, low in LOW_HALVES.items():
        high = low << step
        high = high - (1 << 32) if high >= (1 << 31) else high
        after = pltpu.roll(word, LANES - step, 1)
        before = pltpu.roll(word, step, 1)
        word = jnp.where(
            (lane & step) == 0,
            (word & low) | ((after & low) << step),
            (word & high) | srl(before & high, step),
        )
    count = popcount(word)
    source = lax.broadcasted_iota(jnp.int32, (LANES, LANES), 0)
    target = lax.broadcasted_iota(jnp.int32, (LANES, LANES), 1)
    order = 4 * (source % 32) + source // 32
    ends = exact_dot(count, (order <= target).astype(jnp.float32)).astype(jnp.int32)
    in_range = half * 16 + order // 8 == target % RANGES
    return word, ends, exact_dot(count, in_range.astype(jnp.float32))


def list_hits(halves, position):
    lane = lane_iota(QN)
    (first_word, first_ends, first_hits), (last_word, last_ends, last_hits) = halves
    first_total = jnp.broadcast_to(first_ends[:, LANES - 1 :], (QN, LANES))
    second = lane >= first_total
    wanted = jnp.where(second, lane - first_total, lane)
    found = jnp.zeros((QN, LANES), jnp.int32)
    base = jnp.zeros((QN, LANES), jnp.int32)
    for step in (64, 32, 16, 8, 4, 2, 1):
        index = found + (step - 1)
        count = jnp.where(second, picked(last_ends, index), picked(first_ends, index))
        passed = count <= wanted
        found = jnp.where(passed, found + step, found)
        base = jnp.where(passed, count, base)
    at = 32 * (found & 3) + (found >> 2)
    word = jnp.where(second, picked(last_word, at), picked(first_word, at))
    rank = wanted - base
    bit = jnp.zeros((QN, LANES), jnp.int32)
    for step in (16, 8, 4, 2, 1):
        count = popcount(word & ((1 << step) - 1))
        passed = count <= rank
        rank = jnp.where(passed, rank - count, rank)
        word = jnp.where(passed, srl(word, step), word)
        bit = jnp.where(passed, bit + step, bit)
    local = jnp.where(second, 4096, 0) + 32 * found + bit
    ids = (local >> 8) * ROWS + position * SLICE + (local & (SLICE - 1))
    return ids, (first_hits + last_hits).astype(jnp.int32)


def score_kernel(
    limits_ref,
    words_ref,
    hl0,
    hl1_hbm,
    hl3_hbm,
    far_low_hbm,
    far_high_hbm,
    out0,
    out1,
    out2,
    out3,
    far_low,
    far_high,
    wide_ref,
    hl1,
    hl3,
    hl2,
    onehot_ref,
    lists_ref,
    copied,
):
    moves = ((hl1_hbm, hl1), (hl3_hbm, hl3), (far_low_hbm, far_low), (far_high_hbm, far_high))
    copies = [
        pltpu.make_async_copy(source, target, copied.at[at])
        for at, (source, target) in enumerate(moves)
    ]
    for copy in copies:
        copy.start()
    db, sub = lax.axis_index("db"), lax.axis_index("sub")
    lane = lane_iota(QN)
    mine = 64 * (db % 2) + lax.broadcasted_iota(jnp.int32, (QN, LANES), 0)
    row = jnp.broadcast_to(limits_ref[pl.ds(db // 2, 1), :], (QN, LANES)).astype(jnp.float32)
    limit = jnp.sum(jnp.where(lane == mine, row, 0.0), axis=1, keepdims=True)
    limit = jnp.broadcast_to(limit, (QN, LANES))

    halves = []
    bits = jnp.zeros((QN, LANES), jnp.int32)
    for chunk in range(RANGES * SLICE // CHUNK):
        total = jnp.zeros((2 * QN, CHUNK), jnp.float32)
        for group in range(64 // GROUP):
            shift = (0, 1, 3, 2)[group // 4]
            hl_ref = (hl0, hl1, hl2, hl3)[shift]
            if chunk == 0 and group in (4, 8):
                copies[group // 4 - 1].wait()
            if chunk == 0 and group == 12:
                copies[2].wait()
                copies[3].wait()
                split_tables((far_low, far_high), wide_ref, hl2)
            quarter = (sub + PARTS - shift) % PARTS
            one_hot_group(words_ref, onehot_ref, chunk, quarter, (group % 4) * (GROUP // 4))
            at = (group % 4) * GROUP * K
            total = total + jnp.dot(
                hl_ref[:, at : at + GROUP * K],
                onehot_ref[...],
                preferred_element_type=jnp.float32,
            )
        distance = total[:QN] + total[QN:] * 0.125
        for block in range(CHUNK // LANES):
            matched = distance[:, block * LANES : (block + 1) * LANES] <= limit
            at = (chunk * (CHUNK // LANES) + block) % 32
            bits = bits | jnp.where(matched, (1 << at) if at < 31 else -(1 << 31), 0)
        if (chunk + 1) * CHUNK % 4096 == 0:
            halves.append(hit_words(bits, len(halves)))
            bits = jnp.zeros((QN, LANES), jnp.int32)
    ids, hits = list_hits(halves, sub)
    lists_ref[:, :LANES] = ids
    lists_ref[:, LANES:] = hits
    for shift, out_ref in enumerate((out0, out1, out2, out3)):
        owner = (sub + shift) % PARTS
        out_ref[...] = lists_ref[pl.ds(pl.multiple_of(owner * QB, QB), QB), :]


def merge_kernel(l0, l1, l2, l3, ids_ref, count_ref):
    lane = lane_iota(QB)
    slices = [(lax.axis_index("sub") + PARTS - shift) % PARTS for shift in range(PARTS)]
    refs = (l0, l1, l2, l3)
    counts = jnp.zeros((QB, LANES), jnp.int32)
    for x, ref in zip(slices, refs):
        counts = jnp.where(lane // RANGES == x, ref[:, LANES:], counts)
    source = lax.broadcasted_iota(jnp.int32, (LANES, LANES), 0)
    segment = lax.broadcasted_iota(jnp.int32, (LANES, LANES), 1)
    order = 4 * (source % RANGES) + source // RANGES
    ends = exact_dot(counts, (order <= segment).astype(jnp.float32)).astype(jnp.int32)
    ahead = (order % 4 == segment % 4) & (order < segment)
    skipped = exact_dot(counts, ahead.astype(jnp.float32)).astype(jnp.int32)
    totals = lax.dot_general(
        jnp.ones((8, LANES), jnp.bfloat16),
        counts.astype(jnp.float32).astype(jnp.bfloat16),
        (((1,), (1,)), ((), ())),
        preferred_element_type=jnp.float32,
    )
    found = jnp.zeros((QB, LANES), jnp.int32)
    base = jnp.zeros((QB, LANES), jnp.int32)
    for step, ways in ((16, 8), (4, 4), (1, 4)):
        start = found
        for way in range(1, ways):
            count = picked(ends, start + (way * step - 1))
            passed = count <= lane
            found = jnp.where(passed, start + way * step, found)
            base = jnp.where(passed, count, base)
    valid = lane < jnp.broadcast_to(ends[:, LANES - 1 :], (QB, LANES))
    index = jnp.where(valid, lane - base + picked(skipped, found), 0)
    value = jnp.zeros((QB, LANES), jnp.int32)
    for x, ref in zip(slices, refs):
        value = jnp.where(found % 4 == x, picked(ref[:, :LANES], index), value)
    ids_ref[...] = jnp.where(valid, value, -1)
    count_ref[...] = totals[:1].astype(jnp.int32)


VMEM = pl.BlockSpec(memory_space=pltpu.VMEM)
ANY = pl.BlockSpec(memory_space=pl.ANY)
PARAMS = pltpu.CompilerParams(vmem_limit_bytes=20 * 2**20)


def pack(codes):
    return pl.pallas_call(
        pack_kernel,
        out_shape=jax.ShapeDtypeStruct((RANGES, PARTS * 8, LANES), jnp.int32),
        in_specs=[VMEM],
        out_specs=VMEM,
        compiler_params=PARAMS,
        name="pack",
    )(codes.T)


def split(own, before, after):
    return pl.pallas_call(
        split_kernel,
        out_shape=[jax.ShapeDtypeStruct((2 * QN, 16 * K), F8)] * 3,
        in_specs=[VMEM] * 3,
        out_specs=[VMEM] * 3,
        scratch_shapes=[pltpu.VMEM((2, QN * 16, LANES), jnp.float32)],
        compiler_params=PARAMS,
        name="split",
    )(own, before, after)


def score(limits, words, tabs):
    return pl.pallas_call(
        score_kernel,
        out_shape=[jax.ShapeDtypeStruct((QB, 2 * LANES), jnp.int32)] * PARTS,
        in_specs=[VMEM] * 3 + [ANY] * 4,
        out_specs=[VMEM] * PARTS,
        scratch_shapes=[
            pltpu.VMEM((QN // 2, 16, K), jnp.bfloat16),
            pltpu.VMEM((QN // 2, 16, K), jnp.bfloat16),
            pltpu.VMEM((2, QN * 16, LANES), jnp.float32),
            pltpu.VMEM((2 * QN, 16 * K), F8),
            pltpu.VMEM((2 * QN, 16 * K), F8),
            pltpu.VMEM((2 * QN, 16 * K), F8),
            pltpu.VMEM((GROUP * K, CHUNK), F8),
            pltpu.VMEM((QN, 2 * LANES), jnp.int32),
            pltpu.SemaphoreType.DMA((4,)),
        ],
        compiler_params=PARAMS,
        name="score",
    )(limits, words, *tabs)


def merge(lists):
    return pl.pallas_call(
        merge_kernel,
        out_shape=(
            jax.ShapeDtypeStruct((QB, LANES), jnp.int32),
            jax.ShapeDtypeStruct((1, QB), jnp.int32),
        ),
        in_specs=[VMEM] * PARTS,
        out_specs=(VMEM, VMEM),
        compiler_params=PARAMS,
        name="merge",
    )(*lists)


def shifted(array, by):
    return lax.ppermute(array, "sub", [(x, (x + by) % PARTS) for x in range(PARTS)])


def per_device(codes, tables, limits):
    before, after = shifted(tables, 1), shifted(tables, -1)
    far_low = shifted(before[: QN // 2], 1)
    far_high = shifted(after[QN // 2 :], -1)
    sent = pack(codes).reshape(RANGES * PARTS, 8, LANES)
    words = lax.all_to_all(sent, ("db", "sub"), split_axis=0, concat_axis=0, tiled=True)
    lists = score(
        limits.reshape(16, LANES), words, (*split(tables, before, after), far_low, far_high)
    )
    received = [lists[0]] + [shifted(lists[k], k) for k in range(1, PARTS)]
    ids, count = merge(received)
    return ids, count.reshape(QB)


def solution(mesh):
    placed = (P("db", "sub"), P("db", "sub", None), P())
    return jax.shard_map(
        per_device,
        mesh=mesh,
        in_specs=placed,
        out_specs=(P(("db", "sub"), None), P(("db", "sub"))),
        check_vma=False,
    )
```
